32 devices in a mesh: dp: 4 (over z), seq: 8 (over y, x, core).
Axes of the slice: x: 2, y: 2, z: 4, core: 2. Of those that a mesh axis runs over, the one named last changes fastest.
Arguments:
- tokens: int32 [4, 4096], P('dp', 'seq'), may hold values from 0 to 3
- embed_table: bfloat16 [4, 768], replicated, may hold values from -6 to 6
- mix_weight: bfloat16 [2, 768, 768], replicated, may hold values from -0.21875 to 0.21875
- kernels: bfloat16 [2, 3, 768], replicated, may hold values from -3.5 to 3.5
- donor_proj: bfloat16 [768, 256], replicated, may hold values from -0.21875 to 0.21875
- acceptor_proj: bfloat16 [768, 256], replicated, may hold values from -0.21875 to 0.21875
- tissue_scale: float32 [4, 256], replicated, may hold values from -0.375 to 0.375
- junction_dest: int32 [4, 2048, 1], P('dp', 'seq'), may hold values from 0 to 7; in each aligned block of 256 rows (0 to 255, 256 to 511, ..., all dimensions but the last counted through in order) at most 64 rows name the same one
- donor_offset: int32 [4, 2048], P('dp', 'seq'), may hold values from 0 to 511
- acceptor_offset: int32 [4, 2048], P('dp', 'seq'), may hold values from 0 to 511
- tissue_ids: int32 [4, 2048], P('dp', 'seq'), may hold values from 0 to 3
- targets: float32 [4, 2048], P('dp', 'seq'), may hold values from -6 to 6
Outputs:
- features: bfloat16 [4, 4096, 768], P('dp', 'seq')
- input_grad: bfloat16 [4, 4096, 768], P('dp', 'seq')
- mix_grad: float32 [2, 768, 768], P(None, 'dp')
- kernel_grad: float32 [2, 3, 768], P(None, None, 'dp')
- embed_grad: float32 [4, 768], P(None, 'dp')
- donor_grad: float32 [768, 256], P('dp')
- acceptor_grad: float32 [768, 256], P('dp')
- tissue_grad: float32 [4, 256], P(None, 'dp')
The draws below stay inside these ranges and needn't reach their ends.
Inputs may be any that keep to these rules, and one draw needn't show every extreme that they name: `junction_dest`: in each aligned block of 256 rows (the junctions of one device) no value appears more than 64 times, a bound that some block reaches.
All inputs are finite; a program needn't handle non-finite values.
Results may differ from the reference program's by a relative error of at most 0.02.
Values may be sent and summed in bfloat16 or wider, within the bound.
A program may use at most 64 MiB of HBM per device.

```python
import math
import jax
import jax.numpy as jnp
import numpy as np
from jax import lax

C = 768
E = 256
TISSUES = 4
FIRST_DILATION = 16
SECOND_DILATION = 128
L_DEV = 512
JUNC_DEV = 256
SEQLEN = 4096
EXAMPLES = 4
JUNCS = 2048
CAP = 64
N_SEQ = 8


def set_ends(entries, key, smallest, high):
    longest = entries.shape.index(max(entries.shape))
    spots = []
    for shift in (0, 1):
        where = [jax.random.randint(jax.random.fold_in(key, axis), (), 0, length) for axis, length in enumerate(entries.shape)]
        where[longest] = (where[longest] + shift) % entries.shape[longest]
        spots.append(tuple(where))
    return entries.at[spots[0]].set(smallest).at[spots[1]].set(high)


def level_of(rng, shape, split, least, largest):
    def one(axis_at, parts):
        draws = jax.random.uniform(jax.random.fold_in(jax.random.fold_in(rng, 6), axis_at), (parts,), jnp.float32, least / len(split), largest / len(split))
        return jnp.repeat(jnp.exp(draws), shape[axis_at] // parts).reshape((-1,) + (1,) * (len(shape) - axis_at - 1))

    factor_of = one(*split[0])
    for cut in split[1:]:
        factor_of = factor_of * one(*cut)
    return factor_of


def routed_block(key, own, number, rows, amount, top, reach, skew):
    ranking = jax.random.permutation(key, amount)
    heavy_load, common = shares(amount, rows * top, reach, skew, True), shares(amount, rows * top, reach, skew, False)
    places = jnp.arange(amount)

    def named(lengths, offset_by):
        used = int((lengths > 0).sum())
        fixed = max(1, used // 4)
        passed = fixed + (places - fixed + offset_by * (used - fixed)) % max(1, amount - fixed)
        return jnp.zeros((amount,), jnp.int32).at[ranking[jnp.where(places < fixed, places, passed)]].set(jnp.asarray(lengths, jnp.int32))

    lengths = jnp.where(number % 4 == 0, named(heavy_load, number // 4), named(common, number - number // 4 - 1))
    mixed = jax.random.permutation(jax.random.fold_in(own, 3), amount)
    giver, taker = mixed[0:amount // 2 * 2:2], mixed[1:amount // 2 * 2:2]
    margin = jnp.minimum(lengths[giver] - 1, reach - lengths[taker]) // 2
    margin = jnp.where((giver == ranking[0]) | (taker == ranking[0]) | (lengths[taker] == 0), 0, jnp.maximum(margin, 0))
    passed = jax.random.randint(jax.random.fold_in(own, 4), (amount // 2,), 0, 1 << 20) % (margin + 1)
    lengths = lengths.at[giver].add(-passed).at[taker].add(passed)
    members = jnp.searchsorted(jnp.cumsum(lengths), jnp.arange(rows * top), side="right").astype(jnp.int32)
    listing = members.reshape(top, rows).T
    listing = listing[jax.random.permutation(jax.random.fold_in(own, 1), rows)]
    offset_by = jax.random.randint(jax.random.fold_in(own, 2), (rows, 1), 0, top)
    return jnp.take_along_axis(listing, (jnp.arange(top)[None, :] + offset_by) % top, axis=1)


def shares(amount, total, bound, skew, full):
    loads = [(1 << 20) // math.isqrt(rank ** skew) + 1 for rank in range(1, amount + 1)]
    largest = bound if full else min(bound, max(-(-total // amount), total * loads[0] // sum(loads)))
    least = 1 if total - largest >= amount - 1 else 0
    holding, spare = [largest] + [least] * (amount - 1), total - largest - least * (amount - 1)
    while spare > 0:
        movable = [i for i in range(1, amount) if holding[i] < largest] or [i for i in range(1, amount) if holding[i] < bound]
        mass, budget = sum([loads[i] for i in movable]), spare
        for i in movable:
            addition = min(bound - holding[i], max(1, budget * loads[i] // mass), spare)
            holding[i] = holding[i] + addition
            spare = spare - addition
    return np.array(holding)


def scatter_about(own_key, extent, deviation, limit, split=(), kind=jnp.bfloat16):
    level = level_of(own_key, extent, split, -0.22, 0.18) if split else 1.0
    drawn = jax.random.normal(own_key, extent, jnp.float32) * deviation * level
    return jnp.minimum(jnp.maximum(drawn, -limit), limit).astype(kind)


def setup_inputs(seed: int = 0) -> dict:
    splits = jax.random.split(jax.random.key(seed), 13)
    tokens = set_ends(jax.random.randint(splits[0], (EXAMPLES, SEQLEN), 0, 4), jax.random.fold_in(splits[0], 1), 0, 3).astype(jnp.int32)
    embed_table = scatter_about(splits[1], (4, C), 1.0, 6.0)
    mix_weight = scatter_about(splits[2], (2, C, C), C ** -0.5, 0.21875)
    kernels = scatter_about(splits[3], (2, 3, C), 3 ** -0.5, 3.5)
    donor_proj = scatter_about(splits[4], (C, E), C ** -0.5, 0.21875)
    acceptor_proj = scatter_about(splits[5], (C, E), C ** -0.5, 0.21875)
    tissue_scale = scatter_about(splits[6], (TISSUES, E), E ** -0.5, 0.375, (), jnp.float32)
    junction_dest_keys = jax.random.split(jax.random.fold_in(splits[7], 1), EXAMPLES * JUNCS // JUNC_DEV)
    junction_dest_turns = jax.random.permutation(jax.random.fold_in(splits[7], 3), EXAMPLES * JUNCS // JUNC_DEV)
    junction_dest = jax.vmap(lambda own, number: routed_block(jax.random.fold_in(splits[7], 2), own, number, JUNC_DEV, N_SEQ, 1, CAP, 2))(junction_dest_keys, junction_dest_turns).reshape((EXAMPLES, JUNCS, 1))
    donor_offset = set_ends(jax.random.randint(splits[8], (EXAMPLES, JUNCS), 0, L_DEV), jax.random.fold_in(splits[8], 1), 0, L_DEV - 1).astype(jnp.int32)
    acceptor_offset = set_ends(jax.random.randint(splits[9], (EXAMPLES, JUNCS), 0, L_DEV), jax.random.fold_in(splits[9], 1), 0, L_DEV - 1).astype(jnp.int32)
    tissue_ids = set_ends(jax.random.randint(splits[10], (EXAMPLES, JUNCS), 0, TISSUES), jax.random.fold_in(splits[10], 1), 0, TISSUES - 1).astype(jnp.int32)
    targets = scatter_about(splits[11], (EXAMPLES, JUNCS), 1.0, 6.0, ((0, 4), (1, 8)), jnp.float32)
    return {"tokens": tokens, "embed_table": embed_table, "mix_weight": mix_weight, "kernels": kernels, "donor_proj": donor_proj, "acceptor_proj": acceptor_proj, "tissue_scale": tissue_scale, "junction_dest": junction_dest, "donor_offset": donor_offset, "acceptor_offset": acceptor_offset, "tissue_ids": tissue_ids, "targets": targets}


epsilon = 1e-06

def normalize(stream_wide):
    inv_rms = lax.rsqrt(lax.optimization_barrier(jnp.mean(stream_wide * stream_wide, axis=-1, keepdims=True)) + epsilon)
    return (stream_wide * inv_rms, inv_rms)

def offset_rows(values, distance):
    count = values.shape[0]
    zeros = jnp.zeros((abs(distance),) + values.shape[1:], values.dtype)
    if distance > 0:
        return jnp.concatenate([values[distance:], zeros], 0)
    return jnp.concatenate([zeros, values[:count + distance]], 0)

def gelu_tanh(values):
    return jax.nn.gelu(values, approximate=True)

def reference(tokens, embed_table, mix_weight, kernels, donor_proj, acceptor_proj, tissue_scale, junction_dest, donor_offset, acceptor_offset, tissue_ids, targets):
    dilation_sizes = (FIRST_DILATION, SECOND_DILATION)
    mix_acc = [jnp.zeros((C, C), jnp.float32), jnp.zeros((C, C), jnp.float32)]
    kernel_acc = [jnp.zeros((3, C), jnp.float32), jnp.zeros((3, C), jnp.float32)]
    embed_acc = jnp.zeros((4, C), jnp.float32)
    tissue_acc = jnp.zeros((TISSUES, E), jnp.float32)
    donor_acc = jnp.zeros((C, E), jnp.float32)
    acceptor_accumulator = jnp.zeros((C, E), jnp.float32)
    feature_list = []
    grad_list = []
    for example in range(EXAMPLES):
        tok_row = tokens[example]
        stream = embed_table[tok_row]
        saved = []
        for layer_index in range(2):
            dilation = dilation_sizes[layer_index]
            stream_wide = stream.astype(jnp.float32)
            normed, inv_rms = normalize(stream_wide)
            norm_wide = normed.astype(jnp.bfloat16).astype(jnp.float32)
            kernel_wide = kernels[layer_index].astype(jnp.float32)
            conv_out = kernel_wide[0] * offset_rows(norm_wide, -dilation) + kernel_wide[1] * norm_wide + kernel_wide[2] * offset_rows(norm_wide, dilation)
            activated = gelu_tanh(conv_out).astype(jnp.bfloat16)
            updated_params = stream_wide + jnp.dot(activated, mix_weight[layer_index], preferred_element_type=jnp.float32)
            saved.append((normed, inv_rms, norm_wide, conv_out, activated))
            stream = updated_params.astype(jnp.bfloat16)
        feature_list.append(stream)
        junction_index = jnp.arange(JUNCS, dtype=jnp.int32)
        donor_pos = junction_index // JUNC_DEV * L_DEV + donor_offset[example]
        accept_pos = junction_dest[example, :, 0] * L_DEV + acceptor_offset[example]
        donors = stream[donor_pos]
        accepted = stream[accept_pos]
        donor_emb = jnp.dot(donors, donor_proj, preferred_element_type=jnp.float32)
        accept_emb = jnp.dot(accepted, acceptor_proj, preferred_element_type=jnp.float32).astype(jnp.bfloat16).astype(jnp.float32)
        tissue_rows = tissue_scale[tissue_ids[example]]
        score = lax.optimization_barrier(jnp.sum(donor_emb * accept_emb * tissue_rows, axis=-1))
        misfit = score - targets[example]
        donor_back = (misfit[:, None] * accept_emb * tissue_rows).astype(jnp.bfloat16)
        accept_back = (misfit[:, None] * donor_emb * tissue_rows).astype(jnp.bfloat16)
        tissue_acc = tissue_acc + jax.ops.segment_sum(misfit[:, None] * donor_emb * accept_emb, tissue_ids[example], num_segments=TISSUES)
        donor_acc = donor_acc + jnp.dot(donors.T, donor_back, preferred_element_type=jnp.float32)
        acceptor_accumulator = acceptor_accumulator + jnp.dot(accepted.T, accept_back, preferred_element_type=jnp.float32)
        upstream = jnp.zeros((SEQLEN, C), jnp.float32)
        upstream = upstream.at[donor_pos].add(jnp.dot(donor_back, donor_proj.T, preferred_element_type=jnp.float32))
        upstream = upstream.at[accept_pos].add(jnp.dot(accept_back, acceptor_proj.T, preferred_element_type=jnp.float32))
        for layer_index in (1, 0):
            dilation = dilation_sizes[layer_index]
            normed, inv_rms, norm_wide, conv_out, activated = saved[layer_index]
            upstream_low = upstream.astype(jnp.bfloat16)
            mix_acc[layer_index] = mix_acc[layer_index] + jnp.dot(activated.T, upstream_low, preferred_element_type=jnp.float32)
            act_grad = jnp.dot(upstream_low, mix_weight[layer_index].T, preferred_element_type=jnp.float32)
            gelu_value, pullback = jax.vjp(gelu_tanh, conv_out)
            conv_wide = pullback(act_grad)[0].astype(jnp.bfloat16).astype(jnp.float32)
            kernel_rows = jnp.stack([lax.optimization_barrier(jnp.sum(conv_wide * offset_rows(norm_wide, -dilation), axis=0)), lax.optimization_barrier(jnp.sum(conv_wide * norm_wide, axis=0)), lax.optimization_barrier(jnp.sum(conv_wide * offset_rows(norm_wide, dilation), axis=0))])
            kernel_acc[layer_index] = kernel_acc[layer_index] + kernel_rows
            kernel_wide = kernels[layer_index].astype(jnp.float32)
            norm_grad = kernel_wide[0] * offset_rows(conv_wide, dilation) + kernel_wide[1] * conv_wide + kernel_wide[2] * offset_rows(conv_wide, -dilation)
            upstream = upstream + inv_rms * (norm_grad - normed * lax.optimization_barrier(jnp.mean(norm_grad * normed, axis=-1, keepdims=True)))
        grad_list.append(upstream.astype(jnp.bfloat16))
        embed_acc = embed_acc + jax.ops.segment_sum(upstream, tok_row, num_segments=4)
    features = jnp.stack(feature_list)
    input_grad = jnp.stack(grad_list)
    return (features, input_grad, jnp.stack(mix_acc), jnp.stack(kernel_acc), embed_acc, donor_acc, acceptor_accumulator, tissue_acc)
```

```python
import functools
import math

import jax
import jax.numpy as jnp
from jax import lax
from jax.experimental import pallas as pl
from jax.experimental.pallas import tpu as pltpu
from jax.sharding import PartitionSpec as P

D0 = 16
D1 = 128
EPS = 1e-06
GROUP = 8
COMBOS = 128
ROOT = math.sqrt(2.0 / math.pi)
CUBE = 0.044715
F32 = jnp.float32
BF16 = jnp.bfloat16
MESH = pl.DeviceIdType.MESH


def mm(a, b):
    return lax.dot_general(a, b, (((1,), (0,)), ((), ())), preferred_element_type=F32)


def mm_ta(a, b):
    return lax.dot_general(a, b, (((0,), (0,)), ((), ())), preferred_element_type=F32)


def mm_tb(a, b):
    return lax.dot_general(a, b, (((1,), (1,)), ((), ())), preferred_element_type=F32)


def onehot(cond):
    return jnp.where(cond, 1.0, 0.0).astype(BF16)


def gelu_and_slope(v):
    square = v * v
    t = jnp.tanh(ROOT * (v + CUBE * (square * v)))
    half = 0.5 * (1.0 + t)
    slope = half + (0.5 * ROOT) * v * (1.0 - t * t) * (1.0 + (3.0 * CUBE) * square)
    return v * half, slope


def body(dims, *refs):
    n, m, L, J, C, E, cap, V = dims
    (tok, emb, mix, kern, dproj, aproj, tscale, dest, doff, aoff, tissue, targets) = refs[:12]
    (feat, igrad, mixg, kerng, embg, dong, accg, tisg) = refs[12:20]
    (info_src, info_all, x1, n1e, act, gp1, G, Dm, ans, ret, bb, gq, A, g2, da, dc1e, g1, dc0e,
     gp0, n0l, n0c, n0r, acttT, mt, oh, ohT, n0g, gp0g, inv0g,
     pay, rc, chip, rj, ck, rz, F, sp, rs, s1, rsz, sall, ssem, rsem) = refs[20:]
    me = lax.axis_index("seq")
    q = lax.axis_index("dp")
    groups = n // GROUP
    T = m * groups
    low = lax.rem(me, GROUP)
    base = me - low
    grp = me // GROUP
    b0 = lax.rem(low, 2)
    j0 = low // 2
    rows_q = C // m
    sems = [0]
    sent = []

    def send(src, dst, dp, sq):
        k = sems[0]
        sems[0] += 1
        d = pltpu.make_async_remote_copy(
            src_ref=src, dst_ref=dst, send_sem=ssem.at[k], recv_sem=rsem.at[k],
            device_id=(dp, sq), device_id_type=MESH)
        d.start()
        sent.append(d)
        return d

    def seq_peer(k):
        return lax.rem(me + k, n)

    def low_peer(k):
        return lax.rem(low + k, GROUP)

    def t_peer(k):
        t = lax.rem(q * groups + grp + k, T)
        return t // groups, lax.rem(t, groups)

    barrier = pltpu.get_barrier_semaphore()
    count = 0
    for k in range(1, n):
        pl.semaphore_signal(barrier, inc=1, device_id=(q, seq_peer(k)), device_id_type=MESH)
        count += 1
    for k in range(1, m):
        for g in range(groups):
            pl.semaphore_signal(
                barrier, inc=1,
                device_id=(lax.rem(q + k, m), g * GROUP + low), device_id_type=MESH)
            count += 1
    info_src[...] = jnp.zeros_like(info_src)
    info_src[0:1, :L] = tok[...]
    info_src[1:2, :J] = dest[...]
    info_src[1:2, J:2 * J] = aoff[...]
    info_all[me] = info_src[...]
    pl.semaphore_wait(barrier, count)
    info_cp = [send(info_src, info_all.at[me], q, seq_peer(k)) for k in range(1, n)]

    ew = emb[...].astype(F32)
    inv0 = lax.rsqrt(jnp.mean(ew * ew, axis=-1, keepdims=True) + EPS)
    norm0 = ew * inv0
    n0 = norm0.astype(BF16).astype(F32)
    k0 = kern[0].astype(F32)
    k1 = kern[1].astype(F32)
    idf = lax.broadcasted_iota(jnp.int32, (COMBOS, 1), 0).astype(F32)
    cc = jnp.floor((idf + 0.5) * (1.0 / 25.0))
    rest = idf - 25.0 * cc
    ll = jnp.floor((rest + 0.5) * 0.2)
    rr = rest - 5.0 * ll

    def pick(which, table):
        out = jnp.zeros((COMBOS, table.shape[1]), F32)
        for v in range(V):
            out = out + jnp.where(which == float(v), table[v:v + 1], 0.0)
        return out

    n0l[...] = pick(ll, n0)
    n0c[...] = pick(cc, n0)
    n0r[...] = pick(rr, n0)
    conv0 = k0[0:1] * n0l[...] + k0[1:2] * n0c[...] + k0[2:3] * n0r[...]
    a0, s0 = gelu_and_slope(conv0)
    gp0[...] = s0
    a0 = a0.astype(BF16)
    acttT[...] = a0.astype(F32).T.astype(BF16)
    x1t = (pick(cc, ew) + mm(a0, mix[0])).astype(BF16)
    xw = x1t.astype(F32)
    n1t = (xw * lax.rsqrt(jnp.mean(xw * xw, axis=-1, keepdims=True) + EPS)).astype(BF16)
    invc = pick(cc, jnp.broadcast_to(inv0, (V, 128)))
    lane = lax.broadcasted_iota(jnp.int32, (COMBOS, 128), 1)
    hi = invc.astype(BF16).astype(F32)
    invt = jnp.where(lane == 0, hi, jnp.where(lane == 1, invc - hi, 0.0)).astype(BF16)
    mt[:, :C] = x1t
    mt[:, C:2 * C] = n1t

    upper = onehot(lax.broadcasted_iota(jnp.int32, (J, J), 0) < lax.broadcasted_iota(jnp.int32, (J, J), 1))
    eye = lax.broadcasted_iota(jnp.int32, (J, J), 0) == lax.broadcasted_iota(jnp.int32, (J, J), 1)

    def col(row):
        return jnp.sum(jnp.where(eye, row, 0.0), axis=1, keepdims=True)

    mine = lax.broadcasted_iota(jnp.int32, (n, J), 0) == dest[...]
    before = mm(onehot(mine), upper)
    slot = jnp.sum(jnp.where(mine, before, 0.0), axis=0, keepdims=True)
    place = dest[...].astype(F32) * float(cap) + slot
    Dm[...] = onehot(lax.broadcasted_iota(jnp.int32, (n * cap, J), 0).astype(F32) == place)
    OHd = onehot(lax.broadcasted_iota(jnp.int32, (L, J), 0) == doff[...])
    tcol = col(tissue[...].astype(F32))
    ycol = col(targets[...])

    for cp in info_cp:
        cp.wait_recv()
    lt = jnp.where(me == 0, V, info_all[lax.rem(me + n - 1, n)][0:1, :L])
    rt = jnp.where(me == n - 1, V, info_all[lax.rem(me + 1, n)][0:1, :L])
    te = jnp.concatenate([lt[:, L - 256:], tok[...], rt[:, :256]], axis=1)
    W = L + 2 * D1
    o = 256 - D1
    cen = te[:, o:o + W]
    comb = (cen * 5 + te[:, o - D0:o - D0 + W]) * 5 + te[:, o + D0:o + D0 + W]
    comb = jnp.where(cen == V, 1000, comb)
    hot = jnp.where(lax.broadcasted_iota(jnp.int32, (COMBOS, W), 0) == comb, 1.0, 0.0)
    ohT[...] = hot.astype(BF16)
    oh[...] = hot.T.astype(BF16)

    x1[...] = mm(oh[D1:D1 + L], mt[:, :C]).astype(BF16)
    n1e[...] = mm(oh[...], mt[:, C:2 * C]).astype(BF16)

    R = 32

    @pl.loop(0, L // R)
    def _(i):
        r = pl.multiple_of(i * R, R)
        v = (k1[0:1] * n1e[pl.ds(r, R)].astype(F32) + k1[1:2] * n1e[pl.ds(r + D1, R)].astype(F32)
             + k1[2:3] * n1e[pl.ds(r + 2 * D1, R)].astype(F32))
        a, s = gelu_and_slope(v)
        act[pl.ds(r, R)] = a.astype(BF16)
        gp1[pl.ds(r, R)] = s

    for h in range(2):
        sl = slice(h * L // 2, (h + 1) * L // 2)
        feat[sl] = (x1[sl].astype(F32) + mm(act[sl], mix[1])).astype(BF16)

    rows = [info_all[s][1:2, :] for s in range(n)]
    dests = jnp.concatenate([r[:, :J] for r in rows], axis=0)
    hits = dests == me
    bef = jnp.where(hits, mm(onehot(hits), upper), -1.0)
    for s in range(n):
        pick_s = lax.broadcasted_iota(jnp.int32, (cap, J), 0).astype(F32) == bef[s:s + 1]
        offs = rows[s][:, J:2 * J].astype(F32) + 1.0
        pos = jnp.sum(jnp.where(pick_s, offs, 0.0), axis=1, keepdims=True) - 1.0
        G[s * cap:(s + 1) * cap] = onehot(
            lax.broadcasted_iota(jnp.int32, (cap, L), 1).astype(F32) == pos)
    qx = mm(feat[...], aproj[...]).astype(BF16)
    ans[...] = mm(G[...], qx).astype(BF16).reshape(n, cap, E)
    ans_cp = [send(ans.at[seq_peer(k)], ret.at[me], q, seq_peer(k)) for k in range(1, n)]
    ret[me] = ans[me]

    donors = mm_ta(OHd, feat[...]).astype(BF16)
    pd = mm(donors, dproj[...])
    trow = jnp.zeros((J, E), F32)
    for t in range(tscale.shape[0]):
        trow = trow + jnp.where(tcol == float(t), tscale[t:t + 1], 0.0)
    mid = slice(D1, D1 + L)
    n0g[...] = mm(oh[mid], n0c[...].astype(BF16)).astype(BF16)
    gp0g[...] = mm(oh[mid], gp0[...].astype(BF16)).astype(BF16)
    inv0g[...] = mm(oh[mid], invt)

    for cp in ans_cp:
        cp.wait_recv()
    qj = mm_ta(Dm[...], ret[...].reshape(n * cap, E))
    misfit = jnp.sum(pd * qj * trow, axis=-1, keepdims=True) - ycol
    dP = (misfit * qj * trow).astype(BF16)
    dQ = (misfit * pd * trow).astype(BF16)
    bb[...] = mm(Dm[...], dQ).astype(BF16).reshape(n, cap, E)
    back_cp = [send(bb.at[seq_peer(k)], gq.at[me], q, seq_peer(k)) for k in range(1, n)]
    gq[me] = bb[me]

    tg = misfit * pd * qj
    A[:, :E] = mm(OHd, dP).astype(BF16)
    sp[7] = jnp.zeros_like(sp[7])
    tail = [jnp.sum(jnp.where(tcol == float(t), tg, 0.0), axis=0, keepdims=True)
            for t in range(tscale.shape[0])]
    g2[...] = mm_tb(A[:, :E], dproj[...])

    def weights_half(h):
        a = A[:, h * E:(h + 1) * E]
        for which, left in ((0, act), (4, feat)):
            out = mm_ta(left[...], a).astype(BF16)
            for c in range(E // 128):
                pay[which + h * (E // 128) + c] = out[:, c * 128:(c + 1) * 128]

    weights_half(0)

    for cp in back_cp:
        cp.wait_recv()
    A[:, E:] = mm_ta(G[...], gq[...].reshape(n * cap, E)).astype(BF16)
    g2[...] += mm_tb(A[:, E:], aproj[...])
    da[...] = mm_tb(g2[...].astype(BF16), mix[1])

    def slope_times(i):
        r = pl.multiple_of(i * R, R)
        dc1e[pl.ds(r + D1, R)] = (da[pl.ds(r, R)] * gp1[pl.ds(r, R)]).astype(BF16)

    pl.loop(0, D1 // R)(slope_times)
    pl.loop((L - D1) // R, L // R)(slope_times)
    halo_cp = [
        send(dc1e.at[pl.ds(L, D1)], dc1e.at[pl.ds(0, D1)], q, seq_peer(1)),
        send(dc1e.at[pl.ds(D1, D1)], dc1e.at[pl.ds(L + D1, D1)], q, seq_peer(n - 1)),
    ]
    weights_half(1)
    core_cp = send(pay.at[pl.ds((1 - b0) * 4, 4)], rc, q, me + 1 - 2 * b0)
    pl.loop(D1 // R, (L - D1) // R)(slope_times)

    def kg(i, accs):
        r = pl.multiple_of(i * R, R)
        d = dc1e[pl.ds(r + D1, R)].astype(F32)
        return tuple(
            acc + jnp.sum((d * n1e[pl.ds(r + k * D1, R)].astype(F32)).reshape(R // 8, 8, C), axis=0)
            for k, acc in enumerate(accs))

    kacc = lax.fori_loop(0, L // R, kg, tuple(jnp.zeros((8, C), F32) for _ in range(3)))
    kacc = [jnp.sum(a, axis=0, keepdims=True) for a in kacc]
    zc = jnp.zeros((1, C), F32)
    tail = [jnp.concatenate([t, jnp.zeros((1, C - E), F32)], axis=1) for t in tail]
    extra = jnp.concatenate(kacc + [zc] + tail + [zc] * 8, axis=0)

    for cp in halo_cp:
        cp.wait_recv()

    @pl.when(me == 0)
    def _():
        dc1e[0:D1] = jnp.zeros((D1, C), BF16)

    @pl.when(me == n - 1)
    def _():
        dc1e[L + D1:] = jnp.zeros((D1, C), BF16)

    @pl.loop(0, L // R)
    def _(i):
        r = pl.multiple_of(i * R, R)
        dn = (k1[0:1] * dc1e[pl.ds(r + 2 * D1, R)].astype(F32)
              + k1[1:2] * dc1e[pl.ds(r + D1, R)].astype(F32)
              + k1[2:3] * dc1e[pl.ds(r, R)].astype(F32))
        xx = x1[pl.ds(r, R)].astype(F32)
        inv = lax.rsqrt(jnp.mean(xx * xx, axis=-1, keepdims=True) + EPS)
        nn = xx * inv
        g1[pl.ds(r, R)] = g2[pl.ds(r, R)] + inv * (dn - nn * jnp.mean(dn * nn, axis=-1, keepdims=True))

    S = mm(ohT[:, mid], g1[...].astype(BF16))
    for r in range(7):
        sp[r] = S[r * 16:(r + 1) * 16].astype(BF16)
    sp[7] = extra.astype(BF16)
    srs_cp = [send(sp.at[low_peer(k)], rs.at[k - 1], q, base + low_peer(k)) for k in range(1, GROUP)]

    core_cp.wait_recv()
    for j in range(4):
        chip[j] = (pay[b0 * 4 + j].astype(F32) + rc[j].astype(F32)).astype(BF16)
    chip_cp = []
    for k in range(1, 4):
        jj = lax.rem(j0 + k, 4)
        chip_cp.append(send(chip.at[jj], rj.at[k - 1], q, base + jj * 2 + b0))

    da[...] = mm_tb(g1[...].astype(BF16), mix[0])

    def slope0(i):
        r = pl.multiple_of(i * 16, 16)
        dc0e[pl.ds(r + D0, 16)] = (da[pl.ds(r, 16)] * gp0g[pl.ds(r, 16)].astype(F32)).astype(BF16)

    slope0(0)
    slope0(L // 16 - 1)
    halo0_cp = [
        send(dc0e.at[pl.ds(L, D0)], dc0e.at[pl.ds(0, D0)], q, seq_peer(1)),
        send(dc0e.at[pl.ds(D0, D0)], dc0e.at[pl.ds(L + D0, D0)], q, seq_peer(n - 1)),
    ]
    pl.loop(1, L // 16 - 1)(slope0)

    for cp in srs_cp:
        cp.wait_recv()
    tot = sp[low].astype(F32)
    for k in range(GROUP - 1):
        tot = tot + rs[k].astype(F32)
    s1[...] = tot.astype(BF16)
    sz_cp = []
    for k in range(1, T):
        pq, pg = t_peer(k)
        sz_cp.append(send(s1, rsz.at[k - 1], pq, pg * GROUP + low))

    for cp in chip_cp:
        cp.wait_recv()
    ck[...] = (chip[j0].astype(F32) + rj[0].astype(F32) + rj[1].astype(F32) + rj[2].astype(F32)).astype(BF16)
    z_cp = []
    for k in range(1, T):
        pq, pg = t_peer(k)
        z_cp.append(send(ck.at[pl.ds(pl.multiple_of(pq * rows_q, 16), rows_q)], rz.at[k - 1], pq, pg * GROUP + low))

    for cp in halo0_cp:
        cp.wait_recv()

    @pl.when(me == 0)
    def _():
        dc0e[0:D0] = jnp.zeros((D0, C), BF16)

    @pl.when(me == n - 1)
    def _():
        dc0e[L + D0:] = jnp.zeros((D0, C), BF16)

    for cp in sz_cp:
        cp.wait_recv()
    tot = s1[...].astype(F32)
    for k in range(T - 1):
        tot = tot + rsz[k].astype(F32)
    sall[low] = tot.astype(BF16)
    sag_cp = [send(sall.at[low], sall.at[low], q, base + low_peer(k)) for k in range(1, GROUP)]

    for cp in z_cp:
        cp.wait_recv()
    tot = ck[pl.ds(pl.multiple_of(q * rows_q, 16), rows_q)].astype(F32)
    for k in range(T - 1):
        tot = tot + rz[k].astype(F32)
    p0 = b0 * 4 + j0
    F[p0] = tot.astype(BF16)
    ag_cp = [send(F.at[p0], F.at[p0], q, base + low_peer(k)) for k in range(1, GROUP)]

    @pl.loop(0, L // R)
    def _(i):
        r = pl.multiple_of(i * R, R)
        dn = (k0[0:1] * dc0e[pl.ds(r + 2 * D0, R)].astype(F32)
              + k0[1:2] * dc0e[pl.ds(r + D0, R)].astype(F32)
              + k0[2:3] * dc0e[pl.ds(r, R)].astype(F32))
        nn = n0g[pl.ds(r, R)].astype(F32)
        inv = jnp.sum(inv0g[pl.ds(r, R)], axis=-1, keepdims=True)
        igrad[pl.ds(r, R)] = (
            g1[pl.ds(r, R)] + inv * (dn - nn * jnp.mean(dn * nn, axis=-1, keepdims=True))
        ).astype(BF16)

    for cp in sag_cp:
        cp.wait_recv()
    St = sall[...].reshape(COMBOS, C)
    live = lax.broadcasted_iota(jnp.int32, (COMBOS, C), 0) < 25 * V
    Sm = jnp.where(live, St.astype(F32), 0.0)
    Sb = Sm.astype(BF16)
    mixg[0] = mm(acttT[pl.ds(pl.multiple_of(q * rows_q, 16), rows_q)], Sb)
    Tm = mm_tb(Sb, mix[0]) * gp0[...]

    def own(full, part):
        w = full.shape[1] // m
        out = jnp.zeros((full.shape[0], w), F32)
        for i in range(m):
            out = out + jnp.where(q == i, full[:, i * w:(i + 1) * w], 0.0)
        return out

    kg0 = jnp.concatenate(
        [jnp.sum(t[...] * Tm, axis=0, keepdims=True) for t in (n0l, n0c, n0r)], axis=0)
    kerng[0] = own(kg0, C)
    last = sall[7].astype(F32)
    kerng[1] = own(last[0:3], C)
    tisg[...] = own(last[4:4 + tscale.shape[0], :E], E)
    eg = []
    for v in range(V):
        def total(which, x):
            return jnp.sum(jnp.where(which == float(v), x, 0.0), axis=0, keepdims=True)
        D = k0[0:1] * total(ll, Tm) + k0[1:2] * total(cc, Tm) + k0[2:3] * total(rr, Tm)
        nv = norm0[v:v + 1]
        eg.append(total(cc, Sm) + inv0[v:v + 1] * (D - nv * jnp.mean(D * nv, axis=-1, keepdims=True)))
    embg[...] = own(jnp.concatenate(eg, axis=0), C)

    for cp in ag_cp:
        cp.wait_recv()
    half = E // 128
    md = jnp.concatenate([F[i] for i in range(half)], axis=1)
    ma = jnp.concatenate([F[half + i] for i in range(half)], axis=1)
    mixg[1] = mm_tb(md, dproj[...]) + mm_tb(ma, aproj[...])
    for i in range(half):
        dong[:, i * 128:(i + 1) * 128] = F[4 + i].astype(F32)
        accg[:, i * 128:(i + 1) * 128] = F[4 + half + i].astype(F32)
    for cp in sent:
        cp.wait_send()


def per_device(tokens, embed_table, mix_weight, kernels, donor_proj, acceptor_proj, tissue_scale,
               junction_dest, donor_offset, acceptor_offset, tissue_ids, targets):
    n = lax.axis_size("seq")
    m = lax.axis_size("dp")
    L = tokens.shape[1]
    J = donor_offset.shape[1]
    V, C = embed_table.shape
    E = donor_proj.shape[1]
    cap = 2 * J // n
    groups = n // GROUP
    T = m * groups
    rq = C // m
    W = L + 2 * D1
    vm = pltpu.VMEM
    nsem = 3 * (n - 1) + 4 + 1 + 3 + 2 * (T - 1) + 3 * (GROUP - 1)
    scratch = [
        vm((8, max(L, 2 * J)), jnp.int32), vm((n, 8, max(L, 2 * J)), jnp.int32),
        vm((L, C), BF16), vm((W, C), BF16), vm((L, C), BF16), vm((L, C), F32),
        vm((n * cap, L), BF16), vm((n * cap, J), BF16),
        vm((n, cap, E), BF16), vm((n, cap, E), BF16), vm((n, cap, E), BF16), vm((n, cap, E), BF16),
        vm((L, 2 * E), BF16), vm((L, C), F32), vm((L, C), F32), vm((W, C), BF16),
        vm((L, C), F32), vm((L + 2 * D0, C), BF16),
        vm((COMBOS, C), F32), vm((COMBOS, C), F32), vm((COMBOS, C), F32), vm((COMBOS, C), F32),
        vm((C, COMBOS), BF16), vm((COMBOS, 2 * C), BF16),
        vm((W, COMBOS), BF16), vm((COMBOS, W), BF16),
        vm((L, C), BF16), vm((L, C), BF16), vm((L, 128), F32),
        vm((8, C, 128), BF16), vm((4, C, 128), BF16), vm((4, C, 128), BF16), vm((3, C, 128), BF16),
        vm((C, 128), BF16), vm((T - 1, rq, 128), BF16), vm((8, rq, 128), BF16),
        vm((8, 16, C), BF16), vm((7, 16, C), BF16), vm((16, C), BF16), vm((T - 1, 16, C), BF16),
        vm((8, 16, C), BF16),
        pltpu.SemaphoreType.DMA((nsem,)), pltpu.SemaphoreType.DMA((nsem,)),
    ]
    outs = [
        jax.ShapeDtypeStruct((L, C), BF16), jax.ShapeDtypeStruct((L, C), BF16),
        jax.ShapeDtypeStruct((2, rq, C), F32), jax.ShapeDtypeStruct((2, 3, rq), F32),
        jax.ShapeDtypeStruct((V, rq), F32), jax.ShapeDtypeStruct((rq, E), F32),
        jax.ShapeDtypeStruct((rq, E), F32), jax.ShapeDtypeStruct((tissue_scale.shape[0], E // m), F32),
    ]
    spec = pl.BlockSpec(memory_space=pltpu.VMEM)
    res = pl.pallas_call(
        functools.partial(body, (n, m, L, J, C, E, cap, V)),
        out_shape=outs,
        in_specs=[spec] * 12,
        out_specs=[spec] * 8,
        scratch_shapes=scratch,
        compiler_params=pltpu.CompilerParams(
            collective_id=0, has_side_effects=True, vmem_limit_bytes=56 * 2**20),
        cost_estimate=pl.CostEstimate(flops=6 * 10**9, bytes_accessed=8 * 10**6, transcendentals=10**6),
        name="train_step",
    )(tokens, embed_table, mix_weight, kernels, donor_proj, acceptor_proj, tissue_scale,
      junction_dest.reshape(1, J), donor_offset, acceptor_offset, tissue_ids, targets)
    feat, igrad, *rest = res
    return (feat[None], igrad[None], *rest)


def solution(mesh):
    s = P("dp", "seq")
    placed = (s, P(), P(), P(), P(), P(), P(), P("dp", "seq", None), s, s, s, s)
    return jax.shard_map(
        per_device,
        mesh=mesh,
        in_specs=placed,
        out_specs=(P("dp", "seq", None), P("dp", "seq", None), P(None, "dp", None), P(None, None, "dp"),
                   P(None, "dp"), P("dp", None), P("dp", None), P(None, "dp")),
        check_vma=False,
    )
```

```python
import functools
import math

import jax
import jax.numpy as jnp
from jax import lax
from jax.experimental import pallas as pl
from jax.experimental.pallas import tpu as pltpu
from jax.sharding import PartitionSpec as P

D0 = 16
D1 = 128
EPS = 1e-06
GROUP = 8
COMBOS = 128
ROOT = math.sqrt(2.0 / math.pi)
CUBE = 0.044715
F32 = jnp.float32
BF16 = jnp.bfloat16
MESH = pl.DeviceIdType.MESH


def mm(a, b):
    return lax.dot_general(a, b, (((1,), (0,)), ((), ())), preferred_element_type=F32)


def mm_ta(a, b):
    return lax.dot_general(a, b, (((0,), (0,)), ((), ())), preferred_element_type=F32)


def mm_tb(a, b):
    return lax.dot_general(a, b, (((1,), (1,)), ((), ())), preferred_element_type=F32)


def onehot(cond):
    return jnp.where(cond, 1.0, 0.0).astype(BF16)


def gelu_and_slope(v):
    square = v * v
    t = jnp.tanh(ROOT * (v + CUBE * (square * v)))
    half = 0.5 * (1.0 + t)
    slope = half + (0.5 * ROOT) * v * (1.0 - t * t) * (1.0 + (3.0 * CUBE) * square)
    return v * half, slope


def body(dims, *refs):
    n, m, L, J, C, E, cap, V = dims
    (tok, emb, mix_in, kern, dproj, aproj, tscale, dest, doff, aoff, tissue, targets) = refs[:12]
    (feat_out, igrad, mixg, kerng, embg, dong, accg, tisg) = refs[12:20]
    (info_src, info_all, x1, n1e, act, gp1, G, Dm, ans, ret, bb, gq, A, g2, da, dc1e, g1, dc0e,
     gp0, n0l, n0c, n0r, acttT, mt, oh, ohT, n0g, gp0g, inv0g,
     pay, rc, chip, rj, ck, rz, F, sp, rs, s1, rsz, sall, ssem, rsem, mix, feat, lsem) = refs[20:]
    loads = [pltpu.make_async_copy(mix_in.at[i], mix.at[i], lsem.at[i]) for i in range(2)]
    for cp in loads:
        cp.start()
    store = pltpu.make_async_copy(feat, feat_out, lsem.at[2])
    me = lax.axis_index("seq")
    q = lax.axis_index("dp")
    groups = n // GROUP
    T = m * groups
    low = lax.rem(me, GROUP)
    base = me - low
    grp = me // GROUP
    b0 = lax.rem(low, 2)
    j0 = low // 2
    rows_q = C // m
    sems = [0]
    sent = []

    def send(src, dst, dp, sq):
        k = sems[0]
        sems[0] += 1
        d = pltpu.make_async_remote_copy(
            src_ref=src, dst_ref=dst, send_sem=ssem.at[k], recv_sem=rsem.at[k],
            device_id=(dp, sq), device_id_type=MESH)
        d.start()
        sent.append(d)
        return d

    def seq_peer(k):
        return lax.rem(me + k, n)

    def low_peer(k):
        return lax.rem(low + k, GROUP)

    def t_peer(k):
        t = lax.rem(q * groups + grp + k, T)
        return t // groups, lax.rem(t, groups)

    barrier = pltpu.get_barrier_semaphore()
    count = 0
    for k in range(1, n):
        pl.semaphore_signal(barrier, inc=1, device_id=(q, seq_peer(k)), device_id_type=MESH)
        count += 1
    for k in range(1, m):
        for g in range(groups):
            pl.semaphore_signal(
                barrier, inc=1,
                device_id=(lax.rem(q + k, m), g * GROUP + low), device_id_type=MESH)
            count += 1
    info_src[...] = jnp.zeros_like(info_src)
    info_src[0:1, :L] = tok[...]
    info_src[1:2, :J] = dest[...]
    info_src[1:2, J:2 * J] = aoff[...]
    info_all[me] = info_src[...]
    upper = onehot(lax.broadcasted_iota(jnp.int32, (J, J), 0) < lax.broadcasted_iota(jnp.int32, (J, J), 1))
    eye = lax.broadcasted_iota(jnp.int32, (J, J), 0) == lax.broadcasted_iota(jnp.int32, (J, J), 1)

    def col(row):
        return jnp.sum(jnp.where(eye, row, 0.0), axis=1, keepdims=True)

    mine = lax.broadcasted_iota(jnp.int32, (n, J), 0) == dest[...]
    before = mm(onehot(mine), upper)
    slot = jnp.sum(jnp.where(mine, before, 0.0), axis=0, keepdims=True)
    place = dest[...].astype(F32) * float(cap) + slot
    Dm[...] = onehot(lax.broadcasted_iota(jnp.int32, (n * cap, J), 0).astype(F32) == place)
    OHd = onehot(lax.broadcasted_iota(jnp.int32, (L, J), 0) == doff[...])
    tcol = col(tissue[...].astype(F32))
    ycol = col(targets[...])

    pl.semaphore_wait(barrier, count)
    info_cp = [send(info_src, info_all.at[me], q, seq_peer(k)) for k in range(1, n)]

    loads[0].wait()
    ew = emb[...].astype(F32)
    inv0 = lax.rsqrt(jnp.mean(ew * ew, axis=-1, keepdims=True) + EPS)
    norm0 = ew * inv0
    n0 = norm0.astype(BF16).astype(F32)
    k0 = jnp.concatenate([kern[k].astype(F32)[0:1] for k in range(3)], axis=0)
    k1 = jnp.concatenate([kern[k].astype(F32)[1:2] for k in range(3)], axis=0)
    idf = lax.broadcasted_iota(jnp.int32, (COMBOS, 1), 0).astype(F32)
    cc = jnp.floor((idf + 0.5) * (1.0 / 25.0))
    rest = idf - 25.0 * cc
    ll = jnp.floor((rest + 0.5) * 0.2)
    rr = rest - 5.0 * ll

    def pick(which, table):
        out = jnp.zeros((COMBOS, table.shape[1]), F32)
        for v in range(V):
            out = out + jnp.where(which == float(v), table[v:v + 1], 0.0)
        return out

    n0l[...] = pick(ll, n0)
    n0c[...] = pick(cc, n0)
    n0r[...] = pick(rr, n0)
    conv0 = k0[0:1] * n0l[...] + k0[1:2] * n0c[...] + k0[2:3] * n0r[...]
    a0, s0 = gelu_and_slope(conv0)
    gp0[...] = s0
    a0 = a0.astype(BF16)
    acttT[...] = a0.astype(F32).T.astype(BF16)
    x1t = (pick(cc, ew) + mm(a0, mix[0])).astype(BF16)
    xw = x1t.astype(F32)
    n1t = (xw * lax.rsqrt(jnp.mean(xw * xw, axis=-1, keepdims=True) + EPS)).astype(BF16)
    invc = pick(cc, jnp.broadcast_to(inv0, (V, 128)))
    lane = lax.broadcasted_iota(jnp.int32, (COMBOS, 128), 1)
    hi = invc.astype(BF16).astype(F32)
    invt = jnp.where(lane == 0, hi, jnp.where(lane == 1, invc - hi, 0.0)).astype(BF16)
    mt[:, :C] = x1t
    mt[:, C:2 * C] = n1t

    for cp in info_cp:
        cp.wait_recv()
    lt = jnp.where(me == 0, V, info_all[lax.rem(me + n - 1, n)][0:1, :L])
    rt = jnp.where(me == n - 1, V, info_all[lax.rem(me + 1, n)][0:1, :L])
    te = jnp.concatenate([lt[:, L - 256:], tok[...], rt[:, :256]], axis=1)
    W = L + 2 * D1
    o = 256 - D1
    cen = te[:, o:o + W]
    comb = (cen * 5 + te[:, o - D0:o - D0 + W]) * 5 + te[:, o + D0:o + D0 + W]
    comb = jnp.where(cen == V, 1000, comb)
    hot = jnp.where(lax.broadcasted_iota(jnp.int32, (COMBOS, W), 0) == comb, 1.0, 0.0)
    ohT[...] = hot.astype(BF16)
    oh[...] = hot.T.astype(BF16)

    x1[...] = mm(oh[D1:D1 + L], mt[:, :C]).astype(BF16)
    n1e[...] = mm(oh[...], mt[:, C:2 * C]).astype(BF16)

    R = 32

    @pl.loop(0, L // R)
    def _(i):
        r = pl.multiple_of(i * R, R)
        v = (k1[0:1] * n1e[pl.ds(r, R)].astype(F32) + k1[1:2] * n1e[pl.ds(r + D1, R)].astype(F32)
             + k1[2:3] * n1e[pl.ds(r + 2 * D1, R)].astype(F32))
        a, s = gelu_and_slope(v)
        act[pl.ds(r, R)] = a.astype(BF16)
        gp1[pl.ds(r, R)] = s

    loads[1].wait()
    for h in range(2):
        sl = slice(h * L // 2, (h + 1) * L // 2)
        feat[sl] = (x1[sl].astype(F32) + mm(act[sl], mix[1])).astype(BF16)

    store.start()
    rows = [info_all[s][1:2, :] for s in range(n)]
    dests = jnp.concatenate([r[:, :J] for r in rows], axis=0)
    hits = dests == me
    bef = jnp.where(hits, mm(onehot(hits), upper), -1.0)
    for s in range(n):
        pick_s = lax.broadcasted_iota(jnp.int32, (cap, J), 0).astype(F32) == bef[s:s + 1]
        offs = rows[s][:, J:2 * J].astype(F32) + 1.0
        pos = jnp.sum(jnp.where(pick_s, offs, 0.0), axis=1, keepdims=True) - 1.0
        G[s * cap:(s + 1) * cap] = onehot(
            lax.broadcasted_iota(jnp.int32, (cap, L), 1).astype(F32) == pos)
    qx = mm(feat[...], aproj[...]).astype(BF16)
    ans[...] = mm(G[...], qx).astype(BF16).reshape(n, cap, E)
    ans_cp = [send(ans.at[seq_peer(k)], ret.at[me], q, seq_peer(k)) for k in range(1, n)]
    ret[me] = ans[me]

    donors = mm_ta(OHd, feat[...]).astype(BF16)
    pd = mm(donors, dproj[...])
    trow = jnp.zeros((J, E), F32)
    for t in range(tscale.shape[0]):
        trow = trow + jnp.where(tcol == float(t), tscale[t:t + 1], 0.0)
    mid = slice(D1, D1 + L)
    n0g[...] = mm(oh[mid], n0c[...].astype(BF16)).astype(BF16)
    gp0g[...] = mm(oh[mid], gp0[...].astype(BF16)).astype(BF16)
    inv0g[...] = mm(oh[mid], invt)

    for cp in ans_cp:
        cp.wait_recv()
    qj = mm_ta(Dm[...], ret[...].reshape(n * cap, E))
    misfit = jnp.sum(pd * qj * trow, axis=-1, keepdims=True) - ycol
    dP = (misfit * qj * trow).astype(BF16)
    dQ = (misfit * pd * trow).astype(BF16)
    bb[...] = mm(Dm[...], dQ).astype(BF16).reshape(n, cap, E)
    back_cp = [send(bb.at[seq_peer(k)], gq.at[me], q, seq_peer(k)) for k in range(1, n)]
    gq[me] = bb[me]

    tg = misfit * pd * qj
    A[:, :E] = mm(OHd, dP).astype(BF16)
    sp[7] = jnp.zeros_like(sp[7])
    tail = [jnp.sum(jnp.where(tcol == float(t), tg, 0.0), axis=0, keepdims=True)
            for t in range(tscale.shape[0])]
    g2[...] = mm_tb(A[:, :E], dproj[...])

    hq = rows_q // 2

    def weights_half(h):
        a = A[:, h * E:(h + 1) * E]
        for which, left in ((0, act), (1, feat)):
            out = mm_ta(left[...], a).astype(BF16)
            for c in range(2):
                for b in range(2):
                    for i in range(m):
                        pay[h, b, which * 2 + c, i * hq:(i + 1) * hq] = out[
                            i * rows_q + b * hq:i * rows_q + (b + 1) * hq, c * 128:(c + 1) * 128]
        return send(pay.at[h, 1 - b0], rc.at[h], q, me + 1 - 2 * b0)

    def chip_stage(h, cp):
        cp.wait_recv()
        for j in range(4):
            chip[h, j] = (pay[h, b0, j].astype(F32) + rc[h, j].astype(F32)).astype(BF16)
        out = []
        for k in range(1, 4):
            jj = lax.rem(j0 + k, 4)
            out.append(send(chip.at[h, jj], rj.at[h, k - 1], q, base + jj * 2 + b0))
        return out

    def z_stage(h, cps):
        for cp in cps:
            cp.wait_recv()
        ck[h] = (chip[h, j0].astype(F32) + rj[h, 0].astype(F32) + rj[h, 1].astype(F32)
                 + rj[h, 2].astype(F32)).astype(BF16)
        out = []
        for k in range(1, T):
            pq, pg = t_peer(k)
            out.append(send(ck.at[h, pl.ds(pl.multiple_of(pq * hq, 16), hq)], rz.at[h, k - 1],
                            pq, pg * GROUP + low))
        return out

    def gather_stage(h, cps):
        for cp in cps:
            cp.wait_recv()
        tot = ck[h, pl.ds(pl.multiple_of(q * hq, 16), hq)].astype(F32)
        for k in range(T - 1):
            tot = tot + rz[h, k].astype(F32)
        p0 = b0 * 4 + j0
        F[h, p0] = tot.astype(BF16)
        return [send(F.at[h, p0], F.at[h, p0], q, base + low_peer(k)) for k in range(1, GROUP)]

    core0 = weights_half(0)

    for cp in back_cp:
        cp.wait_recv()
    A[:, E:] = mm_ta(G[...], gq[...].reshape(n * cap, E)).astype(BF16)
    g2[...] += mm_tb(A[:, E:], aproj[...])
    da[...] = mm_tb(g2[...].astype(BF16), mix[1])

    def slope_times(i):
        r = pl.multiple_of(i * R, R)
        dc1e[pl.ds(r + D1, R)] = (da[pl.ds(r, R)] * gp1[pl.ds(r, R)]).astype(BF16)

    pl.loop(0, D1 // R)(slope_times)
    pl.loop((L - D1) // R, L // R)(slope_times)
    halo_cp = [
        send(dc1e.at[pl.ds(L, D1)], dc1e.at[pl.ds(0, D1)], q, seq_peer(1)),
        send(dc1e.at[pl.ds(D1, D1)], dc1e.at[pl.ds(L + D1, D1)], q, seq_peer(n - 1)),
    ]
    chip0 = chip_stage(0, core0)
    core1 = weights_half(1)
    pl.loop(D1 // R, (L - D1) // R)(slope_times)

    def kg(i, accs):
        r = pl.multiple_of(i * R, R)
        d = dc1e[pl.ds(r + D1, R)].astype(F32)
        return tuple(
            acc + jnp.sum((d * n1e[pl.ds(r + k * D1, R)].astype(F32)).reshape(R // 8, 8, C), axis=0)
            for k, acc in enumerate(accs))

    kacc = lax.fori_loop(0, L // R, kg, tuple(jnp.zeros((8, C), F32) for _ in range(3)))
    kacc = [jnp.sum(a, axis=0, keepdims=True) for a in kacc]
    zc = jnp.zeros((1, C), F32)
    tail = [jnp.concatenate([t, jnp.zeros((1, C - E), F32)], axis=1) for t in tail]
    extra = jnp.concatenate(kacc + [zc] + tail + [zc] * 8, axis=0)

    chip1 = chip_stage(1, core1)
    for cp in halo_cp:
        cp.wait_recv()

    @pl.when(me == 0)
    def _():
        dc1e[0:D1] = jnp.zeros((D1, C), BF16)

    @pl.when(me == n - 1)
    def _():
        dc1e[L + D1:] = jnp.zeros((D1, C), BF16)

    @pl.loop(0, L // R)
    def _(i):
        r = pl.multiple_of(i * R, R)
        dn = (k1[0:1] * dc1e[pl.ds(r + 2 * D1, R)].astype(F32)
              + k1[1:2] * dc1e[pl.ds(r + D1, R)].astype(F32)
              + k1[2:3] * dc1e[pl.ds(r, R)].astype(F32))
        xx = x1[pl.ds(r, R)].astype(F32)
        inv = lax.rsqrt(jnp.mean(xx * xx, axis=-1, keepdims=True) + EPS)
        nn = xx * inv
        g1[pl.ds(r, R)] = g2[pl.ds(r, R)] + inv * (dn - nn * jnp.mean(dn * nn, axis=-1, keepdims=True))

    S = mm(ohT[:, mid], g1[...].astype(BF16))
    for r in range(7):
        sp[r] = S[r * 16:(r + 1) * 16].astype(BF16)
    sp[7] = extra.astype(BF16)
    srs_cp = [send(sp.at[low_peer(k)], rs.at[k - 1], q, base + low_peer(k)) for k in range(1, GROUP)]

    z0 = z_stage(0, chip0)
    da[...] = mm_tb(g1[...].astype(BF16), mix[0])

    def slope0(i):
        r = pl.multiple_of(i * 16, 16)
        dc0e[pl.ds(r + D0, 16)] = (da[pl.ds(r, 16)] * gp0g[pl.ds(r, 16)].astype(F32)).astype(BF16)

    slope0(0)
    slope0(L // 16 - 1)
    halo0_cp = [
        send(dc0e.at[pl.ds(L, D0)], dc0e.at[pl.ds(0, D0)], q, seq_peer(1)),
        send(dc0e.at[pl.ds(D0, D0)], dc0e.at[pl.ds(L + D0, D0)], q, seq_peer(n - 1)),
    ]
    pl.loop(1, L // 16 - 1)(slope0)

    for cp in srs_cp:
        cp.wait_recv()
    tot = sp[low].astype(F32)
    for k in range(GROUP - 1):
        tot = tot + rs[k].astype(F32)
    s1[...] = tot.astype(BF16)
    sz_cp = []
    for k in range(1, T):
        pq, pg = t_peer(k)
        sz_cp.append(send(s1, rsz.at[k - 1], pq, pg * GROUP + low))

    z1 = z_stage(1, chip1)
    ag0 = gather_stage(0, z0)

    for cp in halo0_cp:
        cp.wait_recv()

    @pl.when(me == 0)
    def _():
        dc0e[0:D0] = jnp.zeros((D0, C), BF16)

    @pl.when(me == n - 1)
    def _():
        dc0e[L + D0:] = jnp.zeros((D0, C), BF16)

    for cp in sz_cp:
        cp.wait_recv()
    tot = s1[...].astype(F32)
    for k in range(T - 1):
        tot = tot + rsz[k].astype(F32)
    sall[low] = tot.astype(BF16)
    sag_cp = [send(sall.at[low], sall.at[low], q, base + low_peer(k)) for k in range(1, GROUP)]

    ag1 = gather_stage(1, z1)

    @pl.loop(0, L // R)
    def _(i):
        r = pl.multiple_of(i * R, R)
        dn = (k0[0:1] * dc0e[pl.ds(r + 2 * D0, R)].astype(F32)
              + k0[1:2] * dc0e[pl.ds(r + D0, R)].astype(F32)
              + k0[2:3] * dc0e[pl.ds(r, R)].astype(F32))
        nn = n0g[pl.ds(r, R)].astype(F32)
        inv = jnp.sum(inv0g[pl.ds(r, R)], axis=-1, keepdims=True)
        igrad[pl.ds(r, R)] = (
            g1[pl.ds(r, R)] + inv * (dn - nn * jnp.mean(dn * nn, axis=-1, keepdims=True))
        ).astype(BF16)

    for cp in sag_cp:
        cp.wait_recv()
    St = sall[...].reshape(COMBOS, C)
    live = lax.broadcasted_iota(jnp.int32, (COMBOS, C), 0) < 25 * V
    Sm = jnp.where(live, St.astype(F32), 0.0)
    Sb = Sm.astype(BF16)
    mixg[0] = mm(acttT[pl.ds(pl.multiple_of(q * rows_q, 16), rows_q)], Sb)
    Tm = mm_tb(Sb, mix[0]) * gp0[...]

    def own(full, part):
        w = full.shape[1] // m
        out = jnp.zeros((full.shape[0], w), F32)
        for i in range(m):
            out = out + jnp.where(q == i, full[:, i * w:(i + 1) * w], 0.0)
        return out

    kg0 = jnp.concatenate(
        [jnp.sum(t[...] * Tm, axis=0, keepdims=True) for t in (n0l, n0c, n0r)], axis=0)
    last = sall[7].astype(F32)
    kg0 = own(kg0, C)
    kg1 = own(last[0:3], C)
    for k in range(3):
        kerng[k] = jnp.concatenate([kg0[k:k + 1], kg1[k:k + 1]], axis=0)
    tisg[...] = own(last[4:4 + tscale.shape[0], :E], E)
    eg = []
    for v in range(V):
        def total(which, x):
            return jnp.sum(jnp.where(which == float(v), x, 0.0), axis=0, keepdims=True)
        D = k0[0:1] * total(ll, Tm) + k0[1:2] * total(cc, Tm) + k0[2:3] * total(rr, Tm)
        nv = norm0[v:v + 1]
        eg.append(total(cc, Sm) + inv0[v:v + 1] * (D - nv * jnp.mean(D * nv, axis=-1, keepdims=True)))
    embg[...] = own(jnp.concatenate(eg, axis=0), C)

    for cp in ag0 + ag1:
        cp.wait_recv()
    for b in range(2):
        sl = slice(b * hq, (b + 1) * hq)
        md = jnp.concatenate([F[0, b * 4], F[0, b * 4 + 1]], axis=1)
        ma = jnp.concatenate([F[1, b * 4], F[1, b * 4 + 1]], axis=1)
        mixg[1, sl] = mm_tb(md, dproj[...]) + mm_tb(ma, aproj[...])
        for c in range(2):
            dong[sl, c * 128:(c + 1) * 128] = F[0, b * 4 + 2 + c].astype(F32)
            accg[sl, c * 128:(c + 1) * 128] = F[1, b * 4 + 2 + c].astype(F32)
    store.wait()
    for cp in sent:
        cp.wait_send()


def hand_over(*refs):
    held, sem = refs[16:24], refs[24]
    ins = [pltpu.make_async_copy(refs[i], held[i], sem.at[0, i]) for i in range(8)]
    outs = [pltpu.make_async_copy(held[i], refs[8 + i], sem.at[1, i]) for i in range(8)]
    for cp in ins:
        cp.start()
    for i in range(8):
        ins[i].wait()
        outs[i].start()
    for cp in outs:
        cp.wait()


def per_device(tokens, embed_table, mix_weight, kernels, donor_proj, acceptor_proj, tissue_scale,
               junction_dest, donor_offset, acceptor_offset, tissue_ids, targets):
    n = lax.axis_size("seq")
    m = lax.axis_size("dp")
    L = tokens.shape[1]
    J = donor_offset.shape[1]
    V, C = embed_table.shape
    E = donor_proj.shape[1]
    cap = 2 * J // n
    groups = n // GROUP
    T = m * groups
    rq = C // m
    W = L + 2 * D1
    vm = pltpu.VMEM
    nsem = 3 * (n - 1) + 4 + 2 * (1 + 3) + 3 * (T - 1) + 4 * (GROUP - 1)
    scratch = [
        vm((8, max(L, 2 * J)), jnp.int32), vm((n, 8, max(L, 2 * J)), jnp.int32),
        vm((L, C), BF16), vm((W, C), BF16), vm((L, C), BF16), vm((L, C), F32),
        vm((n * cap, L), BF16), vm((n * cap, J), BF16),
        vm((n, cap, E), BF16), vm((n, cap, E), BF16), vm((n, cap, E), BF16), vm((n, cap, E), BF16),
        vm((L, 2 * E), BF16), vm((L, C), F32), vm((L, C), F32), vm((W, C), BF16),
        vm((L, C), F32), vm((L + 2 * D0, C), BF16),
        vm((COMBOS, C), F32), vm((COMBOS, C), F32), vm((COMBOS, C), F32), vm((COMBOS, C), F32),
        vm((C, COMBOS), BF16), vm((COMBOS, 2 * C), BF16),
        vm((W, COMBOS), BF16), vm((COMBOS, W), BF16),
        vm((L, C), BF16), vm((L, C), BF16), vm((L, 128), F32),
        vm((2, 2, 4, C // 2, 128), BF16), vm((2, 4, C // 2, 128), BF16), vm((2, 4, C // 2, 128), BF16),
        vm((2, 3, C // 2, 128), BF16), vm((2, C // 2, 128), BF16), vm((2, T - 1, rq // 2, 128), BF16),
        vm((2, 8, rq // 2, 128), BF16),
        vm((8, 16, C), BF16), vm((7, 16, C), BF16), vm((16, C), BF16), vm((T - 1, 16, C), BF16),
        vm((8, 16, C), BF16),
        pltpu.SemaphoreType.DMA((nsem,)), pltpu.SemaphoreType.DMA((nsem,)),
        vm((2, C, C), BF16), vm((L, C), BF16), pltpu.SemaphoreType.DMA((3,)),
    ]
    outs = [
        jax.ShapeDtypeStruct((L, C), BF16), jax.ShapeDtypeStruct((L, C), BF16),
        jax.ShapeDtypeStruct((2, rq, C), F32), jax.ShapeDtypeStruct((3, 2, rq), F32),
        jax.ShapeDtypeStruct((V, rq), F32), jax.ShapeDtypeStruct((rq, E), F32),
        jax.ShapeDtypeStruct((rq, E), F32), jax.ShapeDtypeStruct((tissue_scale.shape[0], E // m), F32),
    ]
    spec = pl.BlockSpec(memory_space=pltpu.VMEM)
    anywhere = pl.BlockSpec(memory_space=pl.ANY)
    res = pl.pallas_call(
        functools.partial(body, (n, m, L, J, C, E, cap, V)),
        out_shape=outs,
        in_specs=[spec] * 2 + [anywhere] + [spec] * 9,
        out_specs=[anywhere] + [spec] * 7,
        scratch_shapes=scratch,
        compiler_params=pltpu.CompilerParams(
            collective_id=0, has_side_effects=True, vmem_limit_bytes=56 * 2**20),
        cost_estimate=pl.CostEstimate(flops=6 * 10**9, bytes_accessed=8 * 10**6, transcendentals=10**6),
        name="train_step",
    )(tokens, embed_table, mix_weight, kernels.transpose(1, 0, 2), donor_proj, acceptor_proj, tissue_scale,
      junction_dest.reshape(1, J), donor_offset, acceptor_offset, tissue_ids, targets)
    res = pl.pallas_call(
        hand_over,
        out_shape=outs,
        in_specs=[anywhere] * 8,
        out_specs=[anywhere] * 8,
        scratch_shapes=[vm(o.shape, o.dtype) for o in outs] + [pltpu.SemaphoreType.DMA((2, 8))],
        compiler_params=pltpu.CompilerParams(vmem_limit_bytes=16 * 2**20),
        cost_estimate=pl.CostEstimate(flops=0, bytes_accessed=6 * 10**6, transcendentals=0),
        name="hand_over",
    )(*res)
    feat, igrad, mixg, kerng, *rest = res
    return (feat[None], igrad[None], mixg, kerng.transpose(1, 0, 2), *rest)


def solution(mesh):
    s = P("dp", "seq")
    placed = (s, P(), P(), P(), P(), P(), P(), P("dp", "seq", None), s, s, s, s)
    return jax.shard_map(
        per_device,
        mesh=mesh,
        in_specs=placed,
        out_specs=(P("dp", "seq", None), P("dp", "seq", None), P(None, "dp", None), P(None, None, "dp"),
                   P(None, "dp"), P("dp", None), P("dp", None), P(None, "dp")),
        check_vma=False,
    )
```

```python
import functools
import math

import jax
import jax.numpy as jnp
from jax import lax
from jax.experimental import pallas as pl
from jax.experimental.pallas import tpu as pltpu
from jax.sharding import PartitionSpec as P

D0 = 16
D1 = 128
EPS = 1e-06
GROUP = 8
COMBOS = 128
ROOT = math.sqrt(2.0 / math.pi)
CUBE = 0.044715
F32 = jnp.float32
BF16 = jnp.bfloat16
MESH = pl.DeviceIdType.MESH


def mm(a, b):
    return lax.dot_general(a, b, (((1,), (0,)), ((), ())), preferred_element_type=F32)


def mm_ta(a, b):
    return lax.dot_general(a, b, (((0,), (0,)), ((), ())), preferred_element_type=F32)


def mm_tb(a, b):
    return lax.dot_general(a, b, (((1,), (1,)), ((), ())), preferred_element_type=F32)


def onehot(cond):
    return jnp.where(cond, 1.0, 0.0).astype(BF16)


def gelu_and_slope(v):
    square = v * v
    t = jnp.tanh(ROOT * (v + CUBE * (square * v)))
    half = 0.5 * (1.0 + t)
    slope = half + (0.5 * ROOT) * v * (1.0 - t * t) * (1.0 + (3.0 * CUBE) * square)
    return v * half, slope


def body(dims, *refs):
    n, m, L, J, C, E, cap, V = dims
    (tok, emb, mix_in, kern, dproj, aproj, tscale, dest, doff, aoff, tissue, targets) = refs[:12]
    (feat_out, igrad, mixg, kerng, embg, dong, accg, tisg) = refs[12:20]
    (info_src, info_all, x1, n1e, act, gp1, G, Dm, ans, ret, bb, gq, A, g2, da, dc1e, g1, dc0e,
     gp0, n0l, n0c, n0r, acttT, mt, oh, ohT, n0g, gp0g, inv0g,
     pay, rc, chip, rj, ck, rz, F, sp, rs, s1, rsz, sall, ssem, rsem, mix, feat, lsem) = refs[20:]
    loads = [pltpu.make_async_copy(mix_in.at[i], mix.at[i], lsem.at[i]) for i in range(2)]
    for cp in loads:
        cp.start()
    store = pltpu.make_async_copy(feat, feat_out, lsem.at[2])
    me = lax.axis_index("seq")
    q = lax.axis_index("dp")
    groups = n // GROUP
    T = m * groups
    low = lax.rem(me, GROUP)
    base = me - low
    grp = me // GROUP
    b0 = lax.rem(low, 2)
    j0 = low // 2
    rows_q = C // m
    sems = [0]
    sent = []

    def send(src, dst, dp, sq):
        k = sems[0]
        sems[0] += 1
        d = pltpu.make_async_remote_copy(
            src_ref=src, dst_ref=dst, send_sem=ssem.at[k], recv_sem=rsem.at[k],
            device_id=(dp, sq), device_id_type=MESH)
        d.start()
        sent.append(d)
        return d

    def seq_peer(k):
        return lax.rem(me + k, n)

    def low_peer(k):
        return lax.rem(low + k, GROUP)

    def t_peer(k):
        t = lax.rem(q * groups + grp + k, T)
        return t // groups, lax.rem(t, groups)

    barrier = pltpu.get_barrier_semaphore()
    count = 0
    for k in range(1, n):
        pl.semaphore_signal(barrier, inc=1, device_id=(q, seq_peer(k)), device_id_type=MESH)
        count += 1
    for k in range(1, m):
        for g in range(groups):
            pl.semaphore_signal(
                barrier, inc=1,
                device_id=(lax.rem(q + k, m), g * GROUP + low), device_id_type=MESH)
            count += 1
    info_src[...] = jnp.zeros_like(info_src)
    info_src[0:1, :L] = tok[...]
    info_src[1:2, :J] = dest[...]
    info_src[1:2, J:2 * J] = aoff[...]
    info_all[me] = info_src[...]
    upper = onehot(lax.broadcasted_iota(jnp.int32, (J, J), 0) < lax.broadcasted_iota(jnp.int32, (J, J), 1))
    eye = lax.broadcasted_iota(jnp.int32, (J, J), 0) == lax.broadcasted_iota(jnp.int32, (J, J), 1)

    def col(row):
        return jnp.sum(jnp.where(eye, row, 0.0), axis=1, keepdims=True)

    mine = lax.broadcasted_iota(jnp.int32, (n, J), 0) == dest[...]
    before = mm(onehot(mine), upper)
    slot = jnp.sum(jnp.where(mine, before, 0.0), axis=0, keepdims=True)
    place = dest[...].astype(F32) * float(cap) + slot
    Dm[...] = onehot(lax.broadcasted_iota(jnp.int32, (n * cap, J), 0).astype(F32) == place)
    OHd = onehot(lax.broadcasted_iota(jnp.int32, (L, J), 0) == doff[...])
    tcol = col(tissue[...].astype(F32))
    ycol = col(targets[...])

    pl.semaphore_wait(barrier, count)
    info_cp = [send(info_src, info_all.at[me], q, seq_peer(k)) for k in range(1, n)]

    loads[0].wait()
    ew = emb[...].astype(F32)
    inv0 = lax.rsqrt(jnp.mean(ew * ew, axis=-1, keepdims=True) + EPS)
    norm0 = ew * inv0
    n0 = norm0.astype(BF16).astype(F32)
    k0 = jnp.concatenate([kern[k].astype(F32)[0:1] for k in range(3)], axis=0)
    k1 = jnp.concatenate([kern[k].astype(F32)[1:2] for k in range(3)], axis=0)
    idf = lax.broadcasted_iota(jnp.int32, (COMBOS, 1), 0).astype(F32)
    cc = jnp.floor((idf + 0.5) * (1.0 / 25.0))
    rest = idf - 25.0 * cc
    ll = jnp.floor((rest + 0.5) * 0.2)
    rr = rest - 5.0 * ll

    def pick(which, table):
        out = jnp.zeros((COMBOS, table.shape[1]), F32)
        for v in range(V):
            out = out + jnp.where(which == float(v), table[v:v + 1], 0.0)
        return out

    n0l[...] = pick(ll, n0)
    n0c[...] = pick(cc, n0)
    n0r[...] = pick(rr, n0)
    conv0 = k0[0:1] * n0l[...] + k0[1:2] * n0c[...] + k0[2:3] * n0r[...]
    a0, s0 = gelu_and_slope(conv0)
    gp0[...] = s0
    a0 = a0.astype(BF16)
    acttT[...] = a0.astype(F32).T.astype(BF16)
    x1t = (pick(cc, ew) + mm(a0, mix[0])).astype(BF16)
    xw = x1t.astype(F32)
    n1t = (xw * lax.rsqrt(jnp.mean(xw * xw, axis=-1, keepdims=True) + EPS)).astype(BF16)
    invc = pick(cc, jnp.broadcast_to(inv0, (V, 128)))
    lane = lax.broadcasted_iota(jnp.int32, (COMBOS, 128), 1)
    hi = invc.astype(BF16).astype(F32)
    invt = jnp.where(lane == 0, hi, jnp.where(lane == 1, invc - hi, 0.0)).astype(BF16)
    mt[:, :C] = x1t
    mt[:, C:2 * C] = n1t

    for cp in info_cp:
        cp.wait_recv()
    lt = jnp.where(me == 0, V, info_all[lax.rem(me + n - 1, n)][0:1, :L])
    rt = jnp.where(me == n - 1, V, info_all[lax.rem(me + 1, n)][0:1, :L])
    te = jnp.concatenate([lt[:, L - 256:], tok[...], rt[:, :256]], axis=1)
    W = L + 2 * D1
    o = 256 - D1
    cen = te[:, o:o + W]
    comb = (cen * 5 + te[:, o - D0:o - D0 + W]) * 5 + te[:, o + D0:o + D0 + W]
    comb = jnp.where(cen == V, 1000, comb)
    hot = jnp.where(lax.broadcasted_iota(jnp.int32, (COMBOS, W), 0) == comb, 1.0, 0.0)
    ohT[...] = hot.astype(BF16)
    oh[...] = hot.T.astype(BF16)

    x1[...] = mm(oh[D1:D1 + L], mt[:, :C]).astype(BF16)
    n1e[...] = mm(oh[...], mt[:, C:2 * C]).astype(BF16)

    R = 32

    @pl.loop(0, L // R)
    def _(i):
        r = pl.multiple_of(i * R, R)
        v = (k1[0:1] * n1e[pl.ds(r, R)].astype(F32) + k1[1:2] * n1e[pl.ds(r + D1, R)].astype(F32)
             + k1[2:3] * n1e[pl.ds(r + 2 * D1, R)].astype(F32))
        a, s = gelu_and_slope(v)
        act[pl.ds(r, R)] = a.astype(BF16)
        gp1[pl.ds(r, R)] = s

    loads[1].wait()
    for h in range(2):
        sl = slice(h * L // 2, (h + 1) * L // 2)
        feat[sl] = (x1[sl].astype(F32) + mm(act[sl], mix[1])).astype(BF16)

    store.start()
    rows = [info_all[s][1:2, :] for s in range(n)]
    dests = jnp.concatenate([r[:, :J] for r in rows], axis=0)
    hits = dests == me
    bef = jnp.where(hits, mm(onehot(hits), upper), -1.0)
    for s in range(n):
        pick_s = lax.broadcasted_iota(jnp.int32, (cap, J), 0).astype(F32) == bef[s:s + 1]
        offs = rows[s][:, J:2 * J].astype(F32) + 1.0
        pos = jnp.sum(jnp.where(pick_s, offs, 0.0), axis=1, keepdims=True) - 1.0
        G[s * cap:(s + 1) * cap] = onehot(
            lax.broadcasted_iota(jnp.int32, (cap, L), 1).astype(F32) == pos)
    qx = mm(feat[...], aproj[...]).astype(BF16)
    ans[...] = mm(G[...], qx).astype(BF16).reshape(n, cap, E)
    ans_cp = [send(ans.at[seq_peer(k)], ret.at[me], q, seq_peer(k)) for k in range(1, n)]
    ret[me] = ans[me]

    donors = mm_ta(OHd, feat[...]).astype(BF16)
    pd = mm(donors, dproj[...])
    trow = jnp.zeros((J, E), F32)
    for t in range(tscale.shape[0]):
        trow = trow + jnp.where(tcol == float(t), tscale[t:t + 1], 0.0)
    mid = slice(D1, D1 + L)
    n0g[...] = mm(oh[mid], n0c[...].astype(BF16)).astype(BF16)
    gp0g[...] = mm(oh[mid], gp0[...].astype(BF16)).astype(BF16)
    inv0g[...] = mm(oh[mid], invt)

    for cp in ans_cp:
        cp.wait_recv()
    qj = mm_ta(Dm[...], ret[...].reshape(n * cap, E))
    misfit = jnp.sum(pd * qj * trow, axis=-1, keepdims=True) - ycol
    dP = (misfit * qj * trow).astype(BF16)
    dQ = (misfit * pd * trow).astype(BF16)
    bb[...] = mm(Dm[...], dQ).astype(BF16).reshape(n, cap, E)
    back_cp = [send(bb.at[seq_peer(k)], gq.at[me], q, seq_peer(k)) for k in range(1, n)]
    gq[me] = bb[me]

    tg = misfit * pd * qj
    A[:, :E] = mm(OHd, dP).astype(BF16)
    sp[7] = jnp.zeros_like(sp[7])
    tail = [jnp.sum(jnp.where(tcol == float(t), tg, 0.0), axis=0, keepdims=True)
            for t in range(tscale.shape[0])]
    g2[...] = mm_tb(A[:, :E], dproj[...])

    hq = rows_q // 2

    def weights_half(h):
        a = A[:, h * E:(h + 1) * E]
        for which, left in ((0, act), (1, feat)):
            out = mm_ta(left[...], a).astype(BF16)
            for c in range(2):
                for b in range(2):
                    for i in range(m):
                        pay[h, b, which * 2 + c, i * hq:(i + 1) * hq] = out[
                            i * rows_q + b * hq:i * rows_q + (b + 1) * hq, c * 128:(c + 1) * 128]
        return send(pay.at[h, 1 - b0], rc.at[h], q, me + 1 - 2 * b0)

    def chip_stage(h, cp):
        cp.wait_recv()
        for j in range(4):
            chip[h, j] = (pay[h, b0, j].astype(F32) + rc[h, j].astype(F32)).astype(BF16)
        out = []
        for k in range(1, 4):
            jj = lax.rem(j0 + k, 4)
            out.append(send(chip.at[h, jj], rj.at[h, k - 1], q, base + jj * 2 + b0))
        return out

    def z_stage(h, cps):
        for cp in cps:
            cp.wait_recv()
        ck[h] = (chip[h, j0].astype(F32) + rj[h, 0].astype(F32) + rj[h, 1].astype(F32)
                 + rj[h, 2].astype(F32)).astype(BF16)
        out = []
        for k in range(1, T):
            pq, pg = t_peer(k)
            out.append(send(ck.at[h, pl.ds(pl.multiple_of(pq * hq, 16), hq)], rz.at[h, k - 1],
                            pq, pg * GROUP + low))
        return out

    def gather_stage(h, cps):
        for cp in cps:
            cp.wait_recv()
        tot = ck[h, pl.ds(pl.multiple_of(q * hq, 16), hq)].astype(F32)
        for k in range(T - 1):
            tot = tot + rz[h, k].astype(F32)
        p0 = b0 * 4 + j0
        F[h, p0] = tot.astype(BF16)
        return [send(F.at[h, p0], F.at[h, p0], q, base + low_peer(k)) for k in range(1, GROUP)]

    core0 = weights_half(0)

    for cp in back_cp:
        cp.wait_recv()
    A[:, E:] = mm_ta(G[...], gq[...].reshape(n * cap, E)).astype(BF16)
    g2[...] += mm_tb(A[:, E:], aproj[...])
    da[...] = mm_tb(g2[...].astype(BF16), mix[1])

    def slope_times(i):
        r = pl.multiple_of(i * R, R)
        dc1e[pl.ds(r + D1, R)] = (da[pl.ds(r, R)] * gp1[pl.ds(r, R)]).astype(BF16)

    pl.loop(0, D1 // R)(slope_times)
    pl.loop((L - D1) // R, L // R)(slope_times)
    halo_cp = [
        send(dc1e.at[pl.ds(L, D1)], dc1e.at[pl.ds(0, D1)], q, seq_peer(1)),
        send(dc1e.at[pl.ds(D1, D1)], dc1e.at[pl.ds(L + D1, D1)], q, seq_peer(n - 1)),
    ]
    chip0 = chip_stage(0, core0)
    core1 = weights_half(1)
    pl.loop(D1 // R, (L - D1) // R)(slope_times)

    def kg(i, accs):
        r = pl.multiple_of(i * R, R)
        d = dc1e[pl.ds(r + D1, R)].astype(F32)
        return tuple(
            acc + jnp.sum((d * n1e[pl.ds(r + k * D1, R)].astype(F32)).reshape(R // 8, 8, C), axis=0)
            for k, acc in enumerate(accs))

    kacc = lax.fori_loop(0, L // R, kg, tuple(jnp.zeros((8, C), F32) for _ in range(3)))
    kacc = [jnp.sum(a, axis=0, keepdims=True) for a in kacc]
    zc = jnp.zeros((1, C), F32)
    tail = [jnp.concatenate([t, jnp.zeros((1, C - E), F32)], axis=1) for t in tail]
    extra = jnp.concatenate(kacc + [zc] + tail + [zc] * 8, axis=0)

    chip1 = chip_stage(1, core1)
    for cp in halo_cp:
        cp.wait_recv()

    @pl.when(me == 0)
    def _():
        dc1e[0:D1] = jnp.zeros((D1, C), BF16)

    @pl.when(me == n - 1)
    def _():
        dc1e[L + D1:] = jnp.zeros((D1, C), BF16)

    @pl.loop(0, L // R)
    def _(i):
        r = pl.multiple_of(i * R, R)
        dn = (k1[0:1] * dc1e[pl.ds(r + 2 * D1, R)].astype(F32)
              + k1[1:2] * dc1e[pl.ds(r + D1, R)].astype(F32)
              + k1[2:3] * dc1e[pl.ds(r, R)].astype(F32))
        xx = x1[pl.ds(r, R)].astype(F32)
        inv = lax.rsqrt(jnp.mean(xx * xx, axis=-1, keepdims=True) + EPS)
        nn = xx * inv
        g1[pl.ds(r, R)] = g2[pl.ds(r, R)] + inv * (dn - nn * jnp.mean(dn * nn, axis=-1, keepdims=True))

    S = mm(ohT[:, mid], g1[...].astype(BF16))
    for r in range(7):
        sp[r] = S[r * 16:(r + 1) * 16].astype(BF16)
    sp[7] = extra.astype(BF16)
    srs_cp = [send(sp.at[low_peer(k)], rs.at[k - 1], q, base + low_peer(k)) for k in range(1, GROUP)]

    z0 = z_stage(0, chip0)
    da[...] = mm_tb(g1[...].astype(BF16), mix[0])

    def slope0(i):
        r = pl.multiple_of(i * 16, 16)
        dc0e[pl.ds(r + D0, 16)] = (da[pl.ds(r, 16)] * gp0g[pl.ds(r, 16)].astype(F32)).astype(BF16)

    slope0(0)
    slope0(L // 16 - 1)
    halo0_cp = [
        send(dc0e.at[pl.ds(L, D0)], dc0e.at[pl.ds(0, D0)], q, seq_peer(1)),
        send(dc0e.at[pl.ds(D0, D0)], dc0e.at[pl.ds(L + D0, D0)], q, seq_peer(n - 1)),
    ]
    pl.loop(1, L // 16 - 1)(slope0)

    for cp in srs_cp:
        cp.wait_recv()
    tot = sp[low].astype(F32)
    for k in range(GROUP - 1):
        tot = tot + rs[k].astype(F32)
    s1[...] = tot.astype(BF16)
    sz_cp = []
    for k in range(1, T):
        pq, pg = t_peer(k)
        sz_cp.append(send(s1, rsz.at[k - 1], pq, pg * GROUP + low))

    z1 = z_stage(1, chip1)
    ag0 = gather_stage(0, z0)

    for cp in halo0_cp:
        cp.wait_recv()

    @pl.when(me == 0)
    def _():
        dc0e[0:D0] = jnp.zeros((D0, C), BF16)

    @pl.when(me == n - 1)
    def _():
        dc0e[L + D0:] = jnp.zeros((D0, C), BF16)

    for cp in sz_cp:
        cp.wait_recv()
    tot = s1[...].astype(F32)
    for k in range(T - 1):
        tot = tot + rsz[k].astype(F32)
    sall[low] = tot.astype(BF16)
    sag_cp = [send(sall.at[low], sall.at[low], q, base + low_peer(k)) for k in range(1, GROUP)]

    ag1 = gather_stage(1, z1)

    @pl.loop(0, L // R)
    def _(i):
        r = pl.multiple_of(i * R, R)
        dn = (k0[0:1] * dc0e[pl.ds(r + 2 * D0, R)].astype(F32)
              + k0[1:2] * dc0e[pl.ds(r + D0, R)].astype(F32)
              + k0[2:3] * dc0e[pl.ds(r, R)].astype(F32))
        nn = n0g[pl.ds(r, R)].astype(F32)
        inv = jnp.sum(inv0g[pl.ds(r, R)], axis=-1, keepdims=True)
        igrad[pl.ds(r, R)] = (
            g1[pl.ds(r, R)] + inv * (dn - nn * jnp.mean(dn * nn, axis=-1, keepdims=True))
        ).astype(BF16)

    for cp in sag_cp:
        cp.wait_recv()
    St = sall[...].reshape(COMBOS, C)
    live = lax.broadcasted_iota(jnp.int32, (COMBOS, C), 0) < 25 * V
    Sm = jnp.where(live, St.astype(F32), 0.0)
    Sb = Sm.astype(BF16)
    mixg[0] = mm(acttT[pl.ds(pl.multiple_of(q * rows_q, 16), rows_q)], Sb)
    Tm = mm_tb(Sb, mix[0]) * gp0[...]

    def own(full, part):
        w = full.shape[1] // m
        out = jnp.zeros((full.shape[0], w), F32)
        for i in range(m):
            out = out + jnp.where(q == i, full[:, i * w:(i + 1) * w], 0.0)
        return out

    kg0 = jnp.concatenate(
        [jnp.sum(t[...] * Tm, axis=0, keepdims=True) for t in (n0l, n0c, n0r)], axis=0)
    last = sall[7].astype(F32)
    kg0 = own(kg0, C)
    kg1 = own(last[0:3], C)
    for k in range(3):
        kerng[k] = jnp.concatenate([kg0[k:k + 1], kg1[k:k + 1]], axis=0)
    tisg[...] = own(last[4:4 + tscale.shape[0], :E], E)
    eg = []
    for v in range(V):
        def total(which, x):
            return jnp.sum(jnp.where(which == float(v), x, 0.0), axis=0, keepdims=True)
        D = k0[0:1] * total(ll, Tm) + k0[1:2] * total(cc, Tm) + k0[2:3] * total(rr, Tm)
        nv = norm0[v:v + 1]
        eg.append(total(cc, Sm) + inv0[v:v + 1] * (D - nv * jnp.mean(D * nv, axis=-1, keepdims=True)))
    embg[...] = own(jnp.concatenate(eg, axis=0), C)

    for cp in ag0 + ag1:
        cp.wait_recv()
    for b in range(2):
        sl = slice(b * hq, (b + 1) * hq)
        md = jnp.concatenate([F[0, b * 4], F[0, b * 4 + 1]], axis=1)
        ma = jnp.concatenate([F[1, b * 4], F[1, b * 4 + 1]], axis=1)
        mixg[1, sl] = mm_tb(md, dproj[...]) + mm_tb(ma, aproj[...])
        for c in range(2):
            dong[sl, c * 128:(c + 1) * 128] = F[0, b * 4 + 2 + c].astype(F32)
            accg[sl, c * 128:(c + 1) * 128] = F[1, b * 4 + 2 + c].astype(F32)
    store.wait()
    for cp in sent:
        cp.wait_send()


def hand_over(*refs):
    held, sem = refs[16:24], refs[24]
    ins = [pltpu.make_async_copy(refs[i], held[i], sem.at[0, i]) for i in range(8)]
    outs = [pltpu.make_async_copy(held[i], refs[8 + i], sem.at[1, i]) for i in range(8)]
    for cp in ins:
        cp.start()
    for i in range(8):
        ins[i].wait()
        outs[i].start()
    for cp in outs:
        cp.wait()


def per_device(tokens, embed_table, mix_weight, kernels, donor_proj, acceptor_proj, tissue_scale,
               junction_dest, donor_offset, acceptor_offset, tissue_ids, targets):
    n = lax.axis_size("seq")
    m = lax.axis_size("dp")
    L = tokens.shape[1]
    J = donor_offset.shape[1]
    V, C = embed_table.shape
    E = donor_proj.shape[1]
    cap = 2 * J // n
    groups = n // GROUP
    T = m * groups
    rq = C // m
    W = L + 2 * D1
    vm = pltpu.VMEM
    nsem = 3 * (n - 1) + 4 + 2 * (1 + 3) + 3 * (T - 1) + 4 * (GROUP - 1)
    scratch = [
        vm((8, max(L, 2 * J)), jnp.int32), vm((n, 8, max(L, 2 * J)), jnp.int32),
        vm((L, C), BF16), vm((W, C), BF16), vm((L, C), BF16), vm((L, C), F32),
        vm((n * cap, L), BF16), vm((n * cap, J), BF16),
        vm((n, cap, E), BF16), vm((n, cap, E), BF16), vm((n, cap, E), BF16), vm((n, cap, E), BF16),
        vm((L, 2 * E), BF16), vm((L, C), F32), vm((L, C), F32), vm((W, C), BF16),
        vm((L, C), F32), vm((L + 2 * D0, C), BF16),
        vm((COMBOS, C), F32), vm((COMBOS, C), F32), vm((COMBOS, C), F32), vm((COMBOS, C), F32),
        vm((C, COMBOS), BF16), vm((COMBOS, 2 * C), BF16),
        vm((W, COMBOS), BF16), vm((COMBOS, W), BF16),
        vm((L, C), BF16), vm((L, C), BF16), vm((L, 128), F32),
        vm((2, 2, 4, C // 2, 128), BF16), vm((2, 4, C // 2, 128), BF16), vm((2, 4, C // 2, 128), BF16),
        vm((2, 3, C // 2, 128), BF16), vm((2, C // 2, 128), BF16), vm((2, T - 1, rq // 2, 128), BF16),
        vm((2, 8, rq // 2, 128), BF16),
        vm((8, 16, C), BF16), vm((7, 16, C), BF16), vm((16, C), BF16), vm((T - 1, 16, C), BF16),
        vm((8, 16, C), BF16),
        pltpu.SemaphoreType.DMA((nsem,)), pltpu.SemaphoreType.DMA((nsem,)),
        vm((2, C, C), BF16), vm((L, C), BF16), pltpu.SemaphoreType.DMA((3,)),
    ]
    outs = [
        jax.ShapeDtypeStruct((L, C), BF16), jax.ShapeDtypeStruct((L, C), BF16),
        jax.ShapeDtypeStruct((2, rq, C), F32), jax.ShapeDtypeStruct((3, 2, rq), F32),
        jax.ShapeDtypeStruct((V, rq), F32), jax.ShapeDtypeStruct((rq, E), F32),
        jax.ShapeDtypeStruct((rq, E), F32), jax.ShapeDtypeStruct((tissue_scale.shape[0], E // m), F32),
    ]
    spec = pl.BlockSpec(memory_space=pltpu.VMEM)
    anywhere = pl.BlockSpec(memory_space=pl.ANY)
    res = pl.pallas_call(
        functools.partial(body, (n, m, L, J, C, E, cap, V)),
        out_shape=outs,
        in_specs=[spec] * 2 + [anywhere] + [spec] * 9,
        out_specs=[anywhere] + [spec] * 7,
        scratch_shapes=scratch,
        compiler_params=pltpu.CompilerParams(
            collective_id=0, has_side_effects=True, vmem_limit_bytes=56 * 2**20),
        cost_estimate=pl.CostEstimate(flops=6 * 10**9, bytes_accessed=8 * 10**6, transcendentals=10**6),
        name="train_step",
    )(tokens, embed_table, mix_weight, kernels.transpose(1, 0, 2), donor_proj, acceptor_proj, tissue_scale,
      junction_dest.reshape(1, J), donor_offset, acceptor_offset, tissue_ids, targets)
    res = pl.pallas_call(
        hand_over,
        out_shape=outs,
        in_specs=[anywhere] * 8,
        out_specs=[anywhere] * 8,
        scratch_shapes=[vm(o.shape, o.dtype) for o in outs] + [pltpu.SemaphoreType.DMA((2, 8))],
        compiler_params=pltpu.CompilerParams(vmem_limit_bytes=56 * 2**20),
        cost_estimate=pl.CostEstimate(flops=0, bytes_accessed=6 * 10**6, transcendentals=0),
        name="hand_over",
    )(*res)
    feat, igrad, mixg, kerng, *rest = res
    return (feat[None], igrad[None], mixg, kerng.transpose(1, 0, 2), *rest)


def solution(mesh):
    s = P("dp", "seq")
    placed = (s, P(), P(), P(), P(), P(), P(), P("dp", "seq", None), s, s, s, s)
    return jax.shard_map(
        per_device,
        mesh=mesh,
        in_specs=placed,
        out_specs=(P("dp", "seq", None), P("dp", "seq", None), P(None, "dp", None), P(None, None, "dp"),
                   P(None, "dp"), P("dp", None), P("dp", None), P(None, "dp")),
        check_vma=False,
    )
```
